512 devices in a mesh: row: 16 (over y, x), col: 32 (over z, core).
Axes of the slice: x: 4, y: 4, z: 16, core: 2. Of those that a mesh axis runs over, the one named last changes fastest.
Arguments:
- inputs: bfloat16 [1024, 12288], P('col', 'row'), may hold values from -6 to 6
- out_grad: bfloat16 [1024, 24576], P('row', 'col'), may hold values from -6 to 6
- preact: bfloat16 [1024, 24576], P('row', 'col'), may hold values from -5 to 5
- weight: bfloat16 [12288, 24576], P('row', 'col'), may hold values from -0.0546875 to 0.0546875
Outputs:
- input_grad: bfloat16 [1024, 12288], P('col', 'row')
- weight_grad: bfloat16 [12288, 24576], P('row', 'col')
The draws below stay inside these ranges and needn't reach their ends.
All inputs are finite; a program needn't handle non-finite values.
Results may differ from the reference program's by a relative error of at most 0.0049.
Values may be sent and summed in bfloat16 or wider, within the bound.
No kernel may reach another device: no remote copies, remote signals or barrier semaphores. Data moves between devices by JAX's collectives and lax.ppermute only.
A program may use at most 64 MiB of HBM per device.

```python
import jax
import jax.numpy as jnp

D = 12288
FF = 24576
TOKENS = 1024


def strengthened(result, stream_key, source, target, parts, factor):
    owner, partner = [(jnp.arange(result.shape[position]) // (result.shape[position] // parts)).reshape([-1 if axis == position else 1 for axis in range(result.ndim)]) for position in (source, target)]
    chosen = jax.random.permutation(stream_key, parts)[partner]
    strong = (owner == chosen) | (owner == (partner + parts // 2) % parts)
    return jnp.where(strong, factor * result, result)


def shard_levels(key, dims, pieces, least, high):
    def one(axis_at, shards_of):
        draws = jax.random.uniform(jax.random.fold_in(jax.random.fold_in(key, 6), axis_at), (shards_of,), jnp.float32, least / len(pieces), high / len(pieces))
        return jnp.repeat(jnp.exp(draws), dims[axis_at] // shards_of).reshape((-1,) + (1,) * (len(dims) - axis_at - 1))

    factor_of = one(*pieces[0])
    for cut in pieces[1:]:
        factor_of = factor_of * one(*cut)
    return factor_of


def gaussian(stream_key, extent, width, reach, cuts=(), held_as=jnp.bfloat16):
    array = jax.random.normal(stream_key, extent, jnp.float32) * width
    if len(cuts) > 0:
        array = shard_levels(stream_key, extent, cuts, -0.22, 0.18) * array
    return jnp.clip(array, min=-reach, max=reach).astype(held_as)


def bell_draw_with(key, shape, deviation, limit, pieces, heavy, kind=jnp.bfloat16):
    result = deviation * jax.random.normal(key, shape, jnp.float32)
    if pieces:
        result = result * shard_levels(key, shape, pieces, -0.22, 0.18)
    return jnp.clip(strengthened(result, jax.random.fold_in(key, 3), *heavy), -limit, limit).astype(kind)


def setup_inputs(seed: int = 0) -> dict:
    key_of = jax.random.split(jax.random.key(seed), 5)
    return {
        "inputs": gaussian(key_of[0], (TOKENS, D), 1.0, 6.0, ((0, 32), (1, 16))),
        "out_grad": bell_draw_with(key_of[1], (TOKENS, FF), 1.0, 6.0, ((0, 16), (1, 32)), (1, 0, 32, 2.75)),
        "preact": gaussian(key_of[2], (TOKENS, FF), 1.0, 5.0, ((0, 16), (1, 32))),
        "weight": gaussian(key_of[3], (D, FF), D ** -0.5, 0.0546875, ((0, 16), (1, 32))),
    }


def activation_grad(out_grad, preact):
    value = preact.astype(jnp.float32)
    cdf = 0.5 * (1.0 + jax.scipy.special.erf(value * 0.7071067811865476))
    pdf = jnp.exp(-0.5 * value * value) * 0.3989422804014327
    return (out_grad.astype(jnp.float32) * (cdf + value * pdf)).astype(jnp.bfloat16)

def reference(inputs, out_grad, preact, weight):
    act_grad = activation_grad(out_grad, preact)
    weight_grad = (jnp.dot(inputs.T, act_grad, preferred_element_type=jnp.float32) * TOKENS ** (-0.5)).astype(jnp.bfloat16)
    summed = jnp.dot(act_grad, weight.T, preferred_element_type=jnp.float32)
    return (summed.astype(jnp.bfloat16), weight_grad)
```

```python
import jax
import jax.numpy as jnp
from jax import lax
from jax.sharding import Mesh, PartitionSpec as P


def activation_grad(out_grad, preact):
    value = preact.astype(jnp.float32)
    cdf = 0.5 * (1.0 + jax.scipy.special.erf(value * 0.7071067811865476))
    pdf = jnp.exp(-0.5 * value * value) * 0.3989422804014327
    return (out_grad.astype(jnp.float32) * (cdf + value * pdf)).astype(jnp.bfloat16)


def on_device(inputs, out_grad, preact, weight):
    core = lax.axis_index("core")
    swap = [(0, 1), (1, 0)]
    input_all = lax.all_gather(inputs, ("z", "core"), axis=0, tiled=True)
    weight_other = lax.ppermute(weight, "core", swap)

    act = lax.optimization_barrier(activation_grad(out_grad, preact))
    copies = jnp.broadcast_to(act[None], (16,) + act.shape)
    act_all = lax.all_to_all(copies, ("y", "x"), 0, 0, tiled=True)
    tokens = 16 * act.shape[0]
    per = act_all.reshape(16, 2, tokens // 32, act.shape[1])
    mine = lax.dynamic_index_in_dim(per, core, 1, keepdims=False).reshape(tokens // 2, -1)
    theirs = lax.dynamic_index_in_dim(per, 1 - core, 1, keepdims=False).reshape(tokens // 2, -1)
    got = lax.ppermute(theirs, "core", swap)
    dims = (((1,), (1,)), ((), ()))
    terms = lax.dot_general(mine, weight, dims, preferred_element_type=jnp.float32)
    terms = terms + lax.dot_general(got, weight_other, dims, preferred_element_type=jnp.float32)
    sent = terms.astype(jnp.bfloat16)
    parts = lax.all_to_all(sent.reshape(16, tokens // 32, -1), "z", 0, 0, tiled=True)
    input_grad = jnp.sum(parts.astype(jnp.float32), axis=0).astype(jnp.bfloat16)

    weight_sum = lax.dot_general(
        input_all, act_all.reshape(tokens, -1), (((0,), (0,)), ((), ())), preferred_element_type=jnp.float32
    )
    weight_grad = (weight_sum * tokens ** (-0.5)).astype(jnp.bfloat16)
    return input_grad, weight_grad


def solution(mesh):
    fine = Mesh(mesh.devices.reshape(4, 4, 16, 2), ("y", "x", "z", "core"))
    across, along = ("y", "x"), ("z", "core")
    return jax.shard_map(
        on_device,
        mesh=fine,
        in_specs=(P(along, across), P(across, along), P(across, along), P(across, along)),
        out_specs=(P(along, across), P(across, along)),
        check_vma=False,
    )
```

```python
import jax
import jax.numpy as jnp
from jax import lax
from jax.experimental import pallas as pl
from jax.experimental.pallas import tpu as pltpu
from jax.sharding import Mesh, PartitionSpec as P

DEPTH = 16
SWAP = [(0, 1), (1, 0)]
PARITIES = [list(range(0, DEPTH, 2)), list(range(1, DEPTH, 2))]


def activation_grad(out_grad, preact):
    value = preact.astype(jnp.float32)
    cdf = 0.5 * (1.0 + jax.scipy.special.erf(value * 0.7071067811865476))
    pdf = jnp.exp(-0.5 * value * value) * 0.3989422804014327
    return (out_grad.astype(jnp.float32) * (cdf + value * pdf)).astype(jnp.bfloat16)


def hop(x, step):
    pairs = []
    for z in range(DEPTH):
        pairs.append((2 * z, 2 * ((z + step) % DEPTH)))
        pairs.append((2 * z + 1, 2 * ((z - step) % DEPTH) + 1))
    return lax.ppermute(x, ("z", "core"), pairs)


def place(rows, at_ref, held, last, out):
    for j in range(DEPTH):
        source, i = (held, j) if j < DEPTH // 2 else (last, j - DEPTH // 2)
        at = pl.multiple_of(at_ref[j] * rows, rows)
        out[pl.ds(at, rows), :] = source[i * rows : (i + 1) * rows, :]


def placed(at, held, last):
    rows, width = held.shape[0] * 2 // DEPTH, held.shape[1]
    whole = pl.BlockSpec(memory_space=pltpu.VMEM)
    return pl.pallas_call(
        lambda *refs: place(rows, *refs),
        out_shape=jax.ShapeDtypeStruct((DEPTH * rows, width), held.dtype),
        in_specs=[pl.BlockSpec(memory_space=pltpu.SMEM)] + [whole] * 2,
        out_specs=whole,
        cost_estimate=pl.CostEstimate(flops=0, bytes_accessed=1, transcendentals=0),
    )(at, held, last)


def on_device(inputs, out_grad, preact, weight):
    core, z = lax.axis_index("core"), lax.axis_index("z")
    rows, width = inputs.shape[0], weight.shape[1]
    scale = (2 * DEPTH * rows) ** (-0.5)

    def act_of(which):
        part = [lax.dynamic_slice(a, (which * rows, 0), (rows, width)) for a in (out_grad, preact)]
        return activation_grad(*part)

    other = lax.ppermute(lax.optimization_barrier(act_of(1 - core)), "core", SWAP)
    pair = jnp.stack([act_of(core), other])
    copies = lax.optimization_barrier(jnp.broadcast_to(pair[None], (DEPTH,) + pair.shape))
    copies, inputs, weight_sent = lax.optimization_barrier((copies, inputs, weight))
    arrived = lax.all_to_all(copies, ("y", "x"), 0, 0, tiled=True)
    weight_other = lax.ppermute(weight_sent, "core", SWAP)
    held = jnp.concatenate([inputs, hop(inputs, 8)], axis=0)
    held = jnp.concatenate([held, hop(held, 4)], axis=0)

    per = arrived.reshape(DEPTH // 2, 2, 2, rows, width)
    near = z % 2

    def products(parity):
        part = lax.dynamic_slice(per, (0, parity, 0, 0, 0), (DEPTH // 2, 1, 2, rows, width))
        dims = (((1,), (1,)), ((), ()))
        own, theirs = part[:, 0, 0].reshape(-1, width), part[:, 0, 1].reshape(-1, width)
        total = lax.dot_general(own, weight, dims, preferred_element_type=jnp.float32)
        return total + lax.dot_general(theirs, weight_other, dims, preferred_element_type=jnp.float32)

    held, per = lax.optimization_barrier((held, per))
    third = hop(held, 2)
    far = products(1 - near).astype(jnp.bfloat16)
    below = hop(far, 1)
    total = products(near)
    held = jnp.concatenate([held, third], axis=0)
    last = hop(held, 1)
    total = total + below.astype(jnp.float32)
    sent = total.astype(jnp.bfloat16).reshape(DEPTH // 2, rows, -1)
    parts = lax.all_to_all(sent, "z", 0, 0, axis_index_groups=PARITIES, tiled=True)

    turn = jnp.array([int(f"{j:04b}"[::-1], 2) for j in range(DEPTH)], jnp.int32)
    at = (z - (1 - 2 * core) * turn + DEPTH) % DEPTH
    input_mine = placed(at, held, last)
    act_own = arrived[:, 0].reshape(DEPTH * rows, width)
    act_other = arrived[:, 1].reshape(DEPTH * rows, width)
    dims = (((0,), (0,)), ((), ()))
    for_other = lax.dot_general(input_mine, act_other, dims, preferred_element_type=jnp.float32)
    from_other = lax.ppermute((for_other * scale).astype(jnp.bfloat16), "core", SWAP)
    weight_sum = lax.dot_general(input_mine, act_own, dims, preferred_element_type=jnp.float32)
    weight_grad = (weight_sum * scale + from_other.astype(jnp.float32)).astype(jnp.bfloat16)
    input_grad = jnp.sum(parts.astype(jnp.float32), axis=0).astype(jnp.bfloat16)
    return input_grad, weight_grad


def solution(mesh):
    fine = Mesh(mesh.devices.reshape(4, 4, DEPTH, 2), ("y", "x", "z", "core"))
    across, along = ("y", "x"), ("z", "core")
    return jax.shard_map(
        on_device,
        mesh=fine,
        in_specs=(P(along, across), P(across, along), P(across, along), P(across, along)),
        out_specs=(P(along, across), P(across, along)),
        check_vma=False,
    )
```

```python
import jax
import jax.numpy as jnp
from jax import lax
from jax.experimental import pallas as pl
from jax.experimental.pallas import tpu as pltpu
from jax.sharding import Mesh, PartitionSpec as P

DEPTH = 16
SWAP = [(0, 1), (1, 0)]
QUARTERS = [list(range(r, DEPTH, 4)) for r in range(4)]
PARITIES = [list(range(0, DEPTH, 2)), list(range(1, DEPTH, 2))]
WHOLE = pl.BlockSpec(memory_space=pltpu.VMEM)


def activation_grad(out_grad, preact):
    value = preact.astype(jnp.float32)
    cdf = 0.5 * (1.0 + jax.scipy.special.erf(value * 0.7071067811865476))
    pdf = jnp.exp(-0.5 * value * value) * 0.3989422804014327
    return (out_grad.astype(jnp.float32) * (cdf + value * pdf)).astype(jnp.bfloat16)


def after(x, y):
    return lax.optimization_barrier((x, y))[0]


def hop(x, step):
    pairs = []
    for z in range(DEPTH):
        pairs.append((2 * z, 2 * ((z + step) % DEPTH)))
        pairs.append((2 * z + 1, 2 * ((z - step) % DEPTH) + 1))
    return lax.ppermute(x, ("z", "core"), pairs)


def call(kernel, out, *arrays, in_specs=None, out_specs=WHOLE, scratch_shapes=(), flops=1 << 20):
    return pl.pallas_call(
        kernel,
        out_shape=out,
        in_specs=in_specs or [WHOLE] * len(arrays),
        out_specs=out_specs,
        scratch_shapes=scratch_shapes,
        compiler_params=pltpu.CompilerParams(vmem_limit_bytes=32 << 20),
        cost_estimate=pl.CostEstimate(flops=flops, bytes_accessed=1 << 20, transcendentals=0),
    )(*arrays)


def tokens(act, which):
    part = act[:, pl.ds(which, 1)]
    return part.reshape(-1, part.shape[-1])


def tokens_of(act, first, cols):
    parts = [tokens(act, lax.rem(first + k, 4))[:, cols] for k in (0, 2)]
    return jnp.concatenate(parts, axis=0)


def dot(a, b, left, right):
    return lax.dot_general(a, b, (((left,), (right,)), ((), ())), preferred_element_type=jnp.float32)


def terms_kernel(parity, act, weight, weight_other, out):
    part = tokens(act, parity[0])
    width = weight.shape[1]
    total = dot(part[:, :width], weight[...], 1, 1) + dot(part[:, width:], weight_other[...], 1, 1)
    out[...] = total.astype(out.dtype)


def sum_kernel(parts, out):
    out[...] = jnp.sum(parts[...].astype(jnp.float32), axis=0).astype(out.dtype)


def for_other_kernel(scale, quarters, act, near, far, out):
    cols = slice(out.shape[1], None)
    total = dot(near[...], tokens_of(act, quarters[0], cols), 0, 0)
    total = total + dot(far[...], tokens_of(act, quarters[1], cols), 0, 0)
    out[...] = (total * scale).astype(out.dtype)


def own_kernel(scale, quarters, act, near, far, got, out):
    cols = slice(None, out.shape[1])
    total = dot(near[...], tokens_of(act, quarters[0], cols), 0, 0)
    total = total + dot(far[...], tokens_of(act, quarters[1], cols), 0, 0)
    out[...] = (total * scale + got[...].astype(jnp.float32)).astype(out.dtype)


def on_device(inputs, out_grad, preact, weight):
    core, z = lax.axis_index("core"), lax.axis_index("z")
    rows, width = inputs.shape[0], weight.shape[1]
    scale = (2 * DEPTH * rows) ** (-0.5)

    def act_of(which, grad):
        part = [lax.dynamic_slice(a, (which * rows, 0), (rows, width)) for a in (grad, preact)]
        return activation_grad(*part)

    leaving = lax.optimization_barrier(act_of(1 - core, out_grad))
    other = lax.ppermute(leaving, "core", SWAP)
    pair = jnp.concatenate([act_of(core, after(out_grad, leaving)), other], axis=1)
    copies = lax.optimization_barrier(jnp.broadcast_to(pair[None], (DEPTH,) + pair.shape))
    arrived = lax.all_to_all(copies, ("y", "x"), 0, 0, tiled=True)
    weight_other = lax.ppermute(after(weight, copies), "core", SWAP)
    quarter = lax.all_gather(after(inputs, copies), "z", axis=0, axis_index_groups=QUARTERS, tiled=True)
    input_near = jnp.concatenate([quarter, hop(after(quarter, weight_other), 2)], axis=0)
    arrived = after(arrived, quarter)

    act = arrived.reshape(DEPTH // 2, 2, rows, 2 * width)
    near = z % 2
    half = (DEPTH // 2 * rows, inputs.shape[1])
    square = jax.ShapeDtypeStruct(weight.shape, jnp.bfloat16)
    flops = 4 * half[0] * half[1] * width
    scalars = pl.BlockSpec(memory_space=pltpu.SMEM)
    def products(parity, dtype):
        return call(
            terms_kernel,
            jax.ShapeDtypeStruct(half, dtype),
            parity.reshape(1), act, weight, weight_other,
            in_specs=[scalars] + [WHOLE] * 3,
            flops=flops,
        )

    far = products(1 - near, jnp.bfloat16)
    below = hop(far, 1)
    total = products(near, jnp.float32)
    input_far = hop(after(input_near, far), 1)
    sent = (total + below.astype(jnp.float32)).astype(jnp.bfloat16).reshape(DEPTH // 2, rows, -1)
    parts = lax.all_to_all(sent, "z", 0, 0, axis_index_groups=PARITIES, tiled=True)
    input_grad = call(sum_kernel, jax.ShapeDtypeStruct(inputs.shape, jnp.bfloat16), parts)

    act = arrived.reshape(4, 4, rows, 2 * width)
    quarters = jnp.stack([z, z + 3 + 2 * core]) % 4
    held = (quarters, act, input_near)
    for_other = call(
        lambda *refs: for_other_kernel(scale, *refs),
        square, *held, after(input_far, sent),
        in_specs=[scalars] + [WHOLE] * 3,
        flops=2 * flops,
    )
    got = lax.ppermute(for_other, "core", SWAP)
    weight_grad = call(
        lambda *refs: own_kernel(scale, *refs),
        square, *held, input_far, got,
        in_specs=[scalars] + [WHOLE] * 4,
        flops=2 * flops,
    )
    return input_grad, weight_grad


def solution(mesh):
    fine = Mesh(mesh.devices.reshape(4, 4, DEPTH, 2), ("y", "x", "z", "core"))
    across, along = ("y", "x"), ("z", "core")
    return jax.shard_map(
        on_device,
        mesh=fine,
        in_specs=(P(along, across), P(across, along), P(across, along), P(across, along)),
        out_specs=(P(along, across), P(across, along)),
        check_vma=False,
    )
```

```python
import jax
import jax.numpy as jnp
from jax import lax
from jax.experimental import pallas as pl
from jax.experimental.pallas import tpu as pltpu
from jax.sharding import Mesh, PartitionSpec as P

DEPTH = 16
SWAP = [(0, 1), (1, 0)]
QUARTERS = [list(range(r, DEPTH, 4)) for r in range(4)]
PARITIES = [list(range(0, DEPTH, 2)), list(range(1, DEPTH, 2))]
WHOLE = pl.BlockSpec(memory_space=pltpu.VMEM)


def activation_grad(out_grad, preact):
    value = preact.astype(jnp.float32)
    cdf = 0.5 * (1.0 + jax.scipy.special.erf(value * 0.7071067811865476))
    pdf = jnp.exp(-0.5 * value * value) * 0.3989422804014327
    return (out_grad.astype(jnp.float32) * (cdf + value * pdf)).astype(jnp.bfloat16)


def after(x, y):
    return lax.optimization_barrier((x, y))[0]


def hop(x, step):
    pairs = []
    for z in range(DEPTH):
        pairs.append((2 * z, 2 * ((z + step) % DEPTH)))
        pairs.append((2 * z + 1, 2 * ((z - step) % DEPTH) + 1))
    return lax.ppermute(x, ("z", "core"), pairs)


def shift(x, step):
    return lax.ppermute(x, "z", [(z, (z + step) % DEPTH) for z in range(DEPTH)])


def call(kernel, out, *arrays, in_specs=None, out_specs=WHOLE, scratch_shapes=(), flops=1 << 20):
    return pl.pallas_call(
        kernel,
        out_shape=out,
        in_specs=in_specs or [WHOLE] * len(arrays),
        out_specs=out_specs,
        scratch_shapes=scratch_shapes,
        compiler_params=pltpu.CompilerParams(vmem_limit_bytes=32 << 20),
        cost_estimate=pl.CostEstimate(flops=flops, bytes_accessed=1 << 20, transcendentals=0),
    )(*arrays)


def tokens(act, which):
    part = act[:, pl.ds(which, 1)]
    return part.reshape(-1, part.shape[-1])


def tokens_of(act, first, cols):
    parts = [tokens(act, lax.rem(first + k, 4))[:, cols] for k in (0, 2)]
    return jnp.concatenate(parts, axis=0)


def join_kernel(first, second, out):
    rows = first.shape[0]
    out[:rows] = first[...]
    out[rows:] = second[...]


def dot(a, b, left, right):
    return lax.dot_general(a, b, (((left,), (right,)), ((), ())), preferred_element_type=jnp.float32)


def terms_kernel(parity, act, weight, weight_other, out):
    part = tokens(act, parity[0])
    width = weight.shape[1]
    total = dot(part[:, :width], weight[...], 1, 1) + dot(part[:, width:], weight_other[...], 1, 1)
    out[...] = total.astype(out.dtype)


def add_kernel(total, below, out):
    out[...] = (total[...] + below[...].astype(jnp.float32)).astype(out.dtype).reshape(out.shape)


def sum_kernel(parts, out):
    out[...] = jnp.sum(parts[...].astype(jnp.float32), axis=0).astype(out.dtype)


def for_other_kernel(scale, z, act, near, far, out):
    cols = slice(out.shape[1], None)
    total = dot(near[...], tokens_of(act, z[0], cols), 0, 0)
    total = total + dot(far[...], tokens_of(act, z[0] + 1, cols), 0, 0)
    out[...] = (total * scale).astype(out.dtype)


def own_kernel(scale, z, act, near, far, got, out):
    cols = slice(None, out.shape[1])
    total = dot(near[...], tokens_of(act, z[0], cols), 0, 0)
    total = total + dot(far[...], tokens_of(act, z[0] + 1, cols), 0, 0)
    out[...] = (total * scale + got[...].astype(jnp.float32)).astype(out.dtype)


def on_device(inputs, out_grad, preact, weight):
    core, z = lax.axis_index("core"), lax.axis_index("z")
    rows, width = inputs.shape[0], weight.shape[1]
    scale = (2 * DEPTH * rows) ** (-0.5)

    def act_of(which, grad):
        part = [lax.dynamic_slice(a, (which * rows, 0), (rows, width)) for a in (grad, preact)]
        return activation_grad(*part)

    leaving = lax.optimization_barrier(act_of(1 - core, out_grad))
    other = lax.ppermute(leaving, "core", SWAP)
    pair = jnp.concatenate([act_of(core, after(out_grad, leaving)), other], axis=1)
    copies = lax.optimization_barrier(jnp.broadcast_to(pair[None], (DEPTH,) + pair.shape))
    arrived = lax.all_to_all(copies, ("y", "x"), 0, 0, tiled=True)
    weight_other = lax.ppermute(after(weight, copies), "core", SWAP)
    quarter = lax.all_gather(after(inputs, copies), "z", axis=0, axis_index_groups=QUARTERS, tiled=True)
    second = hop(quarter, 2)
    arrived = after(arrived, quarter)

    act = arrived.reshape(DEPTH // 2, 2, rows, 2 * width)
    near = z % 2
    half = (DEPTH // 2 * rows, inputs.shape[1])
    input_near = call(join_kernel, jax.ShapeDtypeStruct(half, inputs.dtype), quarter, second)
    square = jax.ShapeDtypeStruct(weight.shape, jnp.bfloat16)
    flops = 4 * half[0] * half[1] * width
    scalars = pl.BlockSpec(memory_space=pltpu.SMEM)
    def products(parity, dtype):
        return call(
            terms_kernel,
            jax.ShapeDtypeStruct(half, dtype),
            parity.reshape(1), act, weight, weight_other,
            in_specs=[scalars] + [WHOLE] * 3,
            flops=flops,
        )

    far = products(1 - near, jnp.bfloat16)
    below = hop(far, 1)
    total = products(near, jnp.float32)
    input_far = shift(after(input_near, far), -1)
    sent = call(add_kernel, jax.ShapeDtypeStruct((DEPTH // 2, rows, half[1]), jnp.bfloat16), total, below)
    parts = lax.all_to_all(sent, "z", 0, 0, axis_index_groups=PARITIES, tiled=True)
    input_grad = call(sum_kernel, jax.ShapeDtypeStruct(inputs.shape, jnp.bfloat16), parts)

    act = arrived.reshape(4, 4, rows, 2 * width)
    held = (z.reshape(1), act, input_near)
    for_other = call(
        lambda *refs: for_other_kernel(scale, *refs),
        square, *held, after(input_far, sent),
        in_specs=[scalars] + [WHOLE] * 3,
        flops=2 * flops,
    )
    got = lax.ppermute(for_other, "core", SWAP)
    weight_grad = call(
        lambda *refs: own_kernel(scale, *refs),
        square, *held, input_far, got,
        in_specs=[scalars] + [WHOLE] * 4,
        flops=2 * flops,
    )
    return input_grad, weight_grad


def solution(mesh):
    fine = Mesh(mesh.devices.reshape(4, 4, DEPTH, 2), ("y", "x", "z", "core"))
    across, along = ("y", "x"), ("z", "core")
    return jax.shard_map(
        on_device,
        mesh=fine,
        in_specs=(P(along, across), P(across, along), P(across, along), P(across, along)),
        out_specs=(P(along, across), P(across, along)),
        check_vma=False,
    )
```

```python
import jax
import jax.numpy as jnp
from jax import lax
from jax.experimental import pallas as pl
from jax.experimental.pallas import tpu as pltpu
from jax.sharding import Mesh, PartitionSpec as P

DEPTH = 16
SWAP = [(0, 1), (1, 0)]
QUARTERS = [list(range(r, DEPTH, 4)) for r in range(4)]
ORDER = (0, 4, 2, 6, 1, 5, 3, 7)
PARITIES = [[2 * j + p for j in ORDER] for p in (0, 1)]
WHOLE = pl.BlockSpec(memory_space=pltpu.VMEM)


def activation_grad(out_grad, preact):
    value = preact.astype(jnp.float32)
    cdf = 0.5 * (1.0 + jax.scipy.special.erf(value * 0.7071067811865476))
    pdf = jnp.exp(-0.5 * value * value) * 0.3989422804014327
    return (out_grad.astype(jnp.float32) * (cdf + value * pdf)).astype(jnp.bfloat16)


def after(x, y):
    return lax.optimization_barrier((x, y))[0]


def hop(x, step):
    pairs = []
    for z in range(DEPTH):
        pairs.append((2 * z, 2 * ((z + step) % DEPTH)))
        pairs.append((2 * z + 1, 2 * ((z - step) % DEPTH) + 1))
    return lax.ppermute(x, ("z", "core"), pairs)


def shift(x, step):
    return lax.ppermute(x, "z", [(z, (z + step) % DEPTH) for z in range(DEPTH)])


def call(kernel, out, *arrays, in_specs=None, out_specs=WHOLE, scratch_shapes=(), flops=1 << 20):
    return pl.pallas_call(
        kernel,
        out_shape=out,
        in_specs=in_specs or [WHOLE] * len(arrays),
        out_specs=out_specs,
        scratch_shapes=scratch_shapes,
        compiler_params=pltpu.CompilerParams(vmem_limit_bytes=32 << 20),
        cost_estimate=pl.CostEstimate(flops=flops, bytes_accessed=1 << 20, transcendentals=0),
    )(*arrays)


def tokens(act, which):
    part = act[:, pl.ds(which, 1)]
    return part.reshape(-1, part.shape[-1])


def tokens_of(act, first, cols):
    parts = [tokens(act, lax.rem(first + k, 4))[:, cols] for k in (0, 2)]
    return jnp.concatenate(parts, axis=0)


def join_kernel(first, second, out):
    rows = first.shape[0]
    out[:rows] = first[...]
    out[rows:] = second[...]


def dot(a, b, left, right):
    return lax.dot_general(a, b, (((left,), (right,)), ((), ())), preferred_element_type=jnp.float32)


def terms_kernel(parity, act, weight, weight_other, out):
    part = tokens(act, parity[0])
    width = weight.shape[1]
    total = dot(part[:, :width], weight[...], 1, 1) + dot(part[:, width:], weight_other[...], 1, 1)
    out[...] = total.astype(out.dtype)


def add_kernel(total, below, out):
    summed = (total[...] + below[...].astype(jnp.float32)).astype(out.dtype).reshape(out.shape)
    for k, j in enumerate(ORDER):
        out[k] = summed[j]


def sum_kernel(parts, out):
    out[...] = jnp.sum(parts[...].astype(jnp.float32), axis=0).astype(out.dtype)


def for_other_kernel(scale, z, act, near, far, out):
    cols = slice(out.shape[1], None)
    total = dot(near[...], tokens_of(act, z[0], cols), 0, 0)
    total = total + dot(far[...], tokens_of(act, z[0] + 1, cols), 0, 0)
    out[...] = (total * scale).astype(out.dtype)


def own_kernel(scale, z, act, near, far, got, out):
    cols = slice(None, out.shape[1])
    total = dot(near[...], tokens_of(act, z[0], cols), 0, 0)
    total = total + dot(far[...], tokens_of(act, z[0] + 1, cols), 0, 0)
    out[...] = (total * scale + got[...].astype(jnp.float32)).astype(out.dtype)


def on_device(inputs, out_grad, preact, weight):
    core, z = lax.axis_index("core"), lax.axis_index("z")
    rows, width = inputs.shape[0], weight.shape[1]
    scale = (2 * DEPTH * rows) ** (-0.5)

    def act_of(which, grad):
        part = [lax.dynamic_slice(a, (which * rows, 0), (rows, width)) for a in (grad, preact)]
        return activation_grad(*part)

    leaving = lax.optimization_barrier(act_of(1 - core, out_grad))
    other = lax.ppermute(leaving, "core", SWAP)
    pair = jnp.concatenate([act_of(core, after(out_grad, leaving)), other], axis=1)
    copies = lax.optimization_barrier(jnp.broadcast_to(pair[None], (DEPTH,) + pair.shape))
    arrived = lax.all_to_all(copies, ("y", "x"), 0, 0, tiled=True)
    weight_other = lax.ppermute(after(weight, copies), "core", SWAP)
    quarter = lax.all_gather(after(inputs, copies), "z", axis=0, axis_index_groups=QUARTERS, tiled=True)
    second = hop(quarter, 2)
    arrived = after(arrived, quarter)

    act = arrived.reshape(DEPTH // 2, 2, rows, 2 * width)
    near = z % 2
    half = (DEPTH // 2 * rows, inputs.shape[1])
    input_near = call(join_kernel, jax.ShapeDtypeStruct(half, inputs.dtype), quarter, second)
    square = jax.ShapeDtypeStruct(weight.shape, jnp.bfloat16)
    flops = 4 * half[0] * half[1] * width
    scalars = pl.BlockSpec(memory_space=pltpu.SMEM)
    def products(parity, dtype):
        return call(
            terms_kernel,
            jax.ShapeDtypeStruct(half, dtype),
            parity.reshape(1), act, weight, weight_other,
            in_specs=[scalars] + [WHOLE] * 3,
            flops=flops,
        )

    far = products(1 - near, jnp.bfloat16)
    below = hop(far, 1)
    total = products(near, jnp.float32)
    input_far = shift(after(input_near, far), -1)
    sent = call(add_kernel, jax.ShapeDtypeStruct((DEPTH // 2, rows, half[1]), jnp.bfloat16), total, below)
    parts = lax.all_to_all(sent, "z", 0, 0, axis_index_groups=PARITIES, tiled=True)
    input_grad = call(sum_kernel, jax.ShapeDtypeStruct(inputs.shape, jnp.bfloat16), parts)

    act = arrived.reshape(4, 4, rows, 2 * width)
    held = (z.reshape(1), act, input_near)
    for_other = call(
        lambda *refs: for_other_kernel(scale, *refs),
        square, *held, after(input_far, sent),
        in_specs=[scalars] + [WHOLE] * 3,
        flops=2 * flops,
    )
    got = lax.ppermute(for_other, "core", SWAP)
    weight_grad = call(
        lambda *refs: own_kernel(scale, *refs),
        square, *held, input_far, got,
        in_specs=[scalars] + [WHOLE] * 4,
        flops=2 * flops,
    )
    return input_grad, weight_grad


def solution(mesh):
    fine = Mesh(mesh.devices.reshape(4, 4, DEPTH, 2), ("y", "x", "z", "core"))
    across, along = ("y", "x"), ("z", "core")
    return jax.shard_map(
        on_device,
        mesh=fine,
        in_specs=(P(along, across), P(across, along), P(across, along), P(across, along)),
        out_specs=(P(along, across), P(across, along)),
        check_vma=False,
    )
```

```python
import jax
import jax.numpy as jnp
from jax import lax
from jax.experimental import pallas as pl
from jax.experimental.pallas import tpu as pltpu
from jax.sharding import Mesh, PartitionSpec as P

DEPTH = 16
SWAP = [(0, 1), (1, 0)]
QUARTERS = [list(range(r, DEPTH, 4)) for r in range(4)]
ORDER = (0, 4, 2, 6, 1, 5, 3, 7)
PARITIES = [[2 * j + p for j in ORDER] for p in (0, 1)]
WHOLE = pl.BlockSpec(memory_space=pltpu.VMEM)


def activation_grad(out_grad, preact):
    value = preact.astype(jnp.float32)
    cdf = 0.5 * (1.0 + jax.scipy.special.erf(value * 0.7071067811865476))
    pdf = jnp.exp(-0.5 * value * value) * 0.3989422804014327
    return (out_grad.astype(jnp.float32) * (cdf + value * pdf)).astype(jnp.bfloat16)


def after(x, y):
    return lax.optimization_barrier((x, y))[0]


def hop(x, step):
    pairs = []
    for z in range(DEPTH):
        pairs.append((2 * z, 2 * ((z + step) % DEPTH)))
        pairs.append((2 * z + 1, 2 * ((z - step) % DEPTH) + 1))
    return lax.ppermute(x, ("z", "core"), pairs)


def call(kernel, out, *arrays, in_specs=None, out_specs=WHOLE, scratch_shapes=(), flops=1 << 20):
    return pl.pallas_call(
        kernel,
        out_shape=out,
        in_specs=in_specs or [WHOLE] * len(arrays),
        out_specs=out_specs,
        scratch_shapes=scratch_shapes,
        compiler_params=pltpu.CompilerParams(vmem_limit_bytes=32 << 20),
        cost_estimate=pl.CostEstimate(flops=flops, bytes_accessed=1 << 20, transcendentals=0),
    )(*arrays)


def tokens(act, which):
    part = act[:, pl.ds(which, 1)]
    return part.reshape(-1, part.shape[-1])


def tokens_of(act, first, cols):
    parts = [tokens(act, lax.rem(first + k, 4))[:, cols] for k in (0, 2)]
    return jnp.concatenate(parts, axis=0)


def join_kernel(first, second, out):
    rows = first.shape[0]
    out[:rows] = first[...]
    out[rows:] = second[...]


def dot(a, b, left, right):
    return lax.dot_general(a, b, (((left,), (right,)), ((), ())), preferred_element_type=jnp.float32)


def terms_kernel(parity, act, weight, weight_other, out):
    part = tokens(act, parity[0])
    width = weight.shape[1]
    total = dot(part[:, :width], weight[...], 1, 1) + dot(part[:, width:], weight_other[...], 1, 1)
    out[...] = total.astype(out.dtype)


def add_kernel(total, below, out):
    summed = (total[...] + below[...].astype(jnp.float32)).astype(out.dtype).reshape(out.shape)
    for k, j in enumerate(ORDER):
        out[k] = summed[j]


def sum_kernel(parts, out):
    out[...] = jnp.sum(parts[...].astype(jnp.float32), axis=0).astype(out.dtype)


def for_other_kernel(scale, z, core, act, near, far, out):
    cols = slice(out.shape[1], None)
    total = dot(near[...], tokens_of(act, z[0], cols), 0, 0)
    total = total + dot(far[...], tokens_of(act, z[0] + 3 + 2 * core[0], cols), 0, 0)
    out[...] = (total * scale).astype(out.dtype)


def own_kernel(scale, z, core, act, near, far, got, out):
    cols = slice(None, out.shape[1])
    total = dot(near[...], tokens_of(act, z[0], cols), 0, 0)
    total = total + dot(far[...], tokens_of(act, z[0] + 3 + 2 * core[0], cols), 0, 0)
    out[...] = (total * scale + got[...].astype(jnp.float32)).astype(out.dtype)


def on_device(inputs, out_grad, preact, weight):
    core, z = lax.axis_index("core"), lax.axis_index("z")
    rows, width = inputs.shape[0], weight.shape[1]
    scale = (2 * DEPTH * rows) ** (-0.5)

    def act_of(which, grad):
        part = [lax.dynamic_slice(a, (which * rows, 0), (rows, width)) for a in (grad, preact)]
        return activation_grad(*part)

    leaving = lax.optimization_barrier(act_of(1 - core, out_grad))
    other = lax.ppermute(leaving, "core", SWAP)
    pair = jnp.concatenate([act_of(core, after(out_grad, leaving)), other], axis=1)
    copies = lax.optimization_barrier(jnp.broadcast_to(pair[None], (DEPTH,) + pair.shape))
    arrived = lax.all_to_all(copies, ("y", "x"), 0, 0, tiled=True)
    weight_other = lax.ppermute(after(weight, copies), "core", SWAP)
    quarter = lax.all_gather(after(inputs, copies), "z", axis=0, axis_index_groups=QUARTERS, tiled=True)
    second = hop(quarter, 2)
    arrived = after(arrived, quarter)

    act = arrived.reshape(DEPTH // 2, 2, rows, 2 * width)
    near = z % 2
    half = (DEPTH // 2 * rows, inputs.shape[1])
    input_near = call(join_kernel, jax.ShapeDtypeStruct(half, inputs.dtype), quarter, second)
    square = jax.ShapeDtypeStruct(weight.shape, jnp.bfloat16)
    flops = 4 * half[0] * half[1] * width
    scalars = pl.BlockSpec(memory_space=pltpu.SMEM)
    def products(parity, dtype):
        return call(
            terms_kernel,
            jax.ShapeDtypeStruct(half, dtype),
            parity.reshape(1), act, weight, weight_other,
            in_specs=[scalars] + [WHOLE] * 3,
            flops=flops,
        )

    far = products(1 - near, jnp.bfloat16)
    below = hop(far, 1)
    total = products(near, jnp.float32)
    input_far = hop(after(input_near, far), 1)
    sent = call(add_kernel, jax.ShapeDtypeStruct((DEPTH // 2, rows, half[1]), jnp.bfloat16), total, below)
    parts = lax.all_to_all(sent, "z", 0, 0, axis_index_groups=PARITIES, tiled=True)
    input_grad = call(sum_kernel, jax.ShapeDtypeStruct(inputs.shape, jnp.bfloat16), parts)

    act = arrived.reshape(4, 4, rows, 2 * width)
    held = (z.reshape(1), core.reshape(1), act, input_near)
    for_other = call(
        lambda *refs: for_other_kernel(scale, *refs),
        square, *held, after(input_far, sent),
        in_specs=[scalars] * 2 + [WHOLE] * 3,
        flops=2 * flops,
    )
    got = lax.ppermute(for_other, "core", SWAP)
    weight_grad = call(
        lambda *refs: own_kernel(scale, *refs),
        square, *held, input_far, got,
        in_specs=[scalars] * 2 + [WHOLE] * 4,
        flops=2 * flops,
    )
    return input_grad, weight_grad


def solution(mesh):
    fine = Mesh(mesh.devices.reshape(4, 4, DEPTH, 2), ("y", "x", "z", "core"))
    across, along = ("y", "x"), ("z", "core")
    return jax.shard_map(
        on_device,
        mesh=fine,
        in_specs=(P(along, across), P(across, along), P(across, along), P(across, along)),
        out_specs=(P(along, across), P(across, along)),
        check_vma=False,
    )
```
